256 devices in a mesh: box: 64 (over x, z, core), rhs: 4 (over y).
Axes of the slice: x: 4, y: 4, z: 8, core: 2. Of those that a mesh axis runs over, the one named last changes fastest.
Arguments:
- points: bfloat16 [524288, 64], P('box'), may hold values from -6 to 6
- weights: bfloat16 [524288, 128], P('box', 'rhs'), may hold values from -6 to 6
- near_list: int32 [1024, 12], P('box'), may hold values from 0 to 47, as said below
- near_count: int32 [1024], P('box'), may hold values from 1 to 12, as said below
- skeleton_index: int32 [64, 256], P('box'), may hold values from 0 to 8191, as said below
- skeleton_maps: bfloat16 [64, 256, 8192], P('box'), may hold values from -0.0625 to 0.0625
- level_index: int32 [5, 256], replicated, may hold values from 0 to 511, as said below
- level_maps: bfloat16 [5, 256, 512], replicated, may hold values from -0.25 to 0.25
Outputs:
- product: bfloat16 [524288, 128], P('box', 'rhs')
The draws below stay inside these ranges and needn't reach their ends.
Inputs may be any that keep to these rules, and one draw needn't show every extreme that they name: `near_list`: entry k of row g is a slot s naming leaf s % 16 of box g // 16 - 1 + s // 16; that box exists, the entries of a row are distinct, and entry 0 names leaf g itself. Only the first near_count[g] entries of row g of near_list are used; some leaf has 12. `skeleton_index`: distinct within a box. `level_index`: distinct within a row.
All inputs are finite; a program needn't handle non-finite values.
Results may differ from the reference program's by a relative error of at most 0.013.
Values may be sent and summed in bfloat16 or wider, within the bound.
No kernel may reach another device: no remote copies, remote signals or barrier semaphores. Data moves between devices by JAX's collectives and lax.ppermute only.
A program may use at most 192 MiB of HBM per device.

```python
import jax
import jax.numpy as jnp
from jax import lax

DIM = 64
R = 128
S = 256
LEAF = 512
NEAR_MAX = 12
LEAF_DEV = 16
PTS_DEV = 8192
LEAVES = 1024
NPTS = 524288
LEVELS = 6
UPPER = 5
N_BOX = 64


def distinct_with_top(key, total, count):
    first, second = jax.random.split(key)
    rest = jax.random.permutation(first, total - 1)[:count - 1]
    row = jnp.concatenate([jnp.full((1,), total - 1, jnp.int32), rest.astype(jnp.int32)])
    return jax.random.permutation(second, row)


def draw_near_list(key, part):
    key = jax.random.fold_in(key, 11)
    width = 3 * LEAF_DEV
    boxes = LEAVES // LEAF_DEV
    leaf_ids = jnp.arange(LEAVES, dtype=jnp.int32)
    keys = jax.random.split(key, LEAVES)
    shuffled = jax.vmap(lambda k: jax.random.permutation(k, width))(keys).astype(jnp.int32)
    owner_box = (leaf_ids // LEAF_DEV)[:, None] - 1 + shuffled // LEAF_DEV
    usable = (owner_box >= 0) & (owner_box < boxes)
    own_slot = (LEAF_DEV + leaf_ids % LEAF_DEV)[:, None]
    rank = jnp.where(shuffled == own_slot, 0, jnp.where(usable, 1, 2)).astype(jnp.int32)
    order = jnp.argsort(rank, axis=1, stable=True)
    return jnp.take_along_axis(shuffled, order, axis=1)[:, :NEAR_MAX].astype(jnp.int32)


def draw_near_count(key, part):
    key = jax.random.fold_in(key, 12)
    first, second, third = jax.random.split(key, 3)
    boxes = LEAVES // LEAF_DEV
    density = jax.random.randint(first, (boxes,), 2, NEAR_MAX + 1)
    raw = jax.random.randint(second, (LEAVES,), 0, 1 << 20)
    counts = raw % jnp.repeat(density, LEAF_DEV) + 1
    forced = jax.random.randint(third, (), 0, LEAVES)
    return jnp.where(jnp.arange(LEAVES) == forced, NEAR_MAX, counts).astype(jnp.int32)


def draw_skeleton_index(key, part):
    key = jax.random.fold_in(key, 13)
    boxes = LEAVES // LEAF_DEV
    keys = jax.random.split(key, boxes)
    return jax.vmap(lambda k: distinct_with_top(k, PTS_DEV, S))(keys).astype(jnp.int32)


def draw_level_index(key, part):
    key = jax.random.fold_in(key, 14)
    keys = jax.random.split(key, UPPER)
    return jax.vmap(lambda k: distinct_with_top(k, 2 * S, S))(keys).astype(jnp.int32)


def block_levels(stream_key, dims, cuts, least, largest):
    factor_of, own = 1.0, jax.random.fold_in(stream_key, 6)
    for axis_at, blocks in cuts:
        draws = jnp.exp(jax.random.uniform(jax.random.fold_in(own, axis_at), (blocks,), jnp.float32, least / len(cuts), largest / len(cuts)))
        factor_of = factor_of * jnp.repeat(draws, dims[axis_at] // blocks).reshape([-1 if axis == axis_at else 1 for axis in range(len(dims))])
    return factor_of


def normal_values(rng, dims, deviation, reach, pieces=(), held_as=jnp.bfloat16):
    result = deviation * jax.random.normal(rng, dims, jnp.float32)
    if pieces:
        result = result * block_levels(rng, dims, pieces, -0.22, 0.18)
    return jnp.clip(result, -reach, reach).astype(held_as)


def setup_inputs(seed: int = 0) -> dict:
    arg_keys = jax.random.split(jax.random.key(seed), 9)
    points = normal_values(arg_keys[0], (NPTS, DIM), 1.0, 6.0, ((0, 64),))
    weights = normal_values(arg_keys[1], (NPTS, R), 1.0, 6.0, ((0, 64), (1, 4)))
    near_list = draw_near_list(jax.random.fold_in(arg_keys[8], 71), 0)
    near_count = draw_near_count(jax.random.fold_in(arg_keys[8], 71), 0)
    skeleton_index = draw_skeleton_index(jax.random.fold_in(arg_keys[8], 71), 0)
    skeleton_maps = normal_values(arg_keys[5], (N_BOX, S, PTS_DEV), PTS_DEV ** -0.5, 0.0625, ((0, 64),))
    level_index = draw_level_index(jax.random.fold_in(arg_keys[8], 71), 0)
    level_maps = normal_values(arg_keys[7], (UPPER, S, 2 * S), (2 * S) ** -0.5, 0.25)
    return dict(points=points, weights=weights, near_list=near_list, near_count=near_count, skeleton_index=skeleton_index, skeleton_maps=skeleton_maps, level_index=level_index, level_maps=level_maps)


def kernel_apply(rows, centers, values):
    rows_wide = rows.astype(jnp.float32)
    cent_wide = centers.astype(jnp.float32)
    dist = jnp.sum(rows_wide * rows_wide, axis=1)[:, None] + jnp.sum(cent_wide * cent_wide, axis=1)[None, :]
    dist = dist - 2.0 * jnp.dot(rows, centers.T, preferred_element_type=jnp.float32)
    kern = jnp.exp(dist * (-2.0 / rows.shape[1])).astype(jnp.bfloat16)
    return jnp.dot(kern, values, preferred_element_type=jnp.float32)


def reference(points, weights, near_list, near_count, skeleton_index, skeleton_maps, level_index, level_maps):
    boxes = LEAVES // LEAF_DEV
    leaf_pts = points.reshape(LEAVES, LEAF, DIM)
    leaf_wts = weights.reshape(LEAVES, LEAF, R)

    def one_leaf(leaf_id):
        base = leaf_id - leaf_id % LEAF_DEV - LEAF_DEV

        def pair(k, total):
            target = (base + near_list[leaf_id, k]).astype(jnp.int32)
            block = kernel_apply(leaf_pts[leaf_id], leaf_pts[target], leaf_wts[target])
            return total + jnp.where(k < near_count[leaf_id], block, jnp.zeros_like(block))

        return lax.fori_loop(0, NEAR_MAX, pair, jnp.zeros((LEAF, R), jnp.float32))

    near = lax.map(one_leaf, jnp.arange(LEAVES, dtype=jnp.int32)).reshape(NPTS, R)

    box_pts = points.reshape(boxes, PTS_DEV, DIM)
    box_wts = weights.reshape(boxes, PTS_DEV, R)
    coords = jnp.take_along_axis(box_pts, skeleton_index[:, :, None].astype(jnp.int32), axis=1)
    values = jnp.einsum("bsp,bpr->bsr", skeleton_maps.astype(jnp.float32), box_wts.astype(jnp.float32)).astype(jnp.bfloat16)
    far = jnp.zeros((boxes, PTS_DEV, R), jnp.float32)
    box_ids = jnp.arange(boxes, dtype=jnp.int32)
    for level in range(LEVELS):
        def one_box(box_id, coords=coords, values=values, level=level):
            other = jnp.bitwise_xor(jnp.right_shift(box_id, level), 1)
            return kernel_apply(box_pts[box_id], coords[other], values[other])

        far = far + lax.map(one_box, box_ids)
        if level < LEVELS - 1:
            count = coords.shape[0] // 2
            union_c = coords.reshape(count, 2 * S, DIM)
            union_v = values.reshape(count, 2 * S, R)
            coords = union_c[:, level_index[level], :]
            values = jnp.einsum("st,ntr->nsr", level_maps[level].astype(jnp.float32), union_v.astype(jnp.float32)).astype(jnp.bfloat16)
    return (near + far.reshape(NPTS, R)).astype(jnp.bfloat16)
```

```python
import functools

import jax
import jax.numpy as jnp
from jax import lax
from jax.experimental import pallas as pl
from jax.experimental.pallas import tpu as pltpu
from jax.sharding import PartitionSpec as P

LEAF = 512
HALF = 256
UNROLL = 16
AHEAD = 2
LIST = 512
DEPTH = 128
ROW_BITS = 5
VMEM = 40 * 2**20
F32 = jnp.float32
BF16 = jnp.bfloat16
NT = (((1,), (1,)), ((), ()))
TN = (((0,), (0,)), ((), ()))


def in_vmem():
    return pl.BlockSpec(memory_space=pltpu.VMEM)


def in_smem():
    return pl.BlockSpec(memory_space=pltpu.SMEM)


def params():
    return pltpu.CompilerParams(vmem_limit_bytes=VMEM)


def write_lists(near_list, near_count, lists, counts, far_blocks):
    leaves, slots = near_list.shape
    first_far = 2 * leaves
    for seg in range(3):
        counts[seg] = 0

    def leaf_body(leaf, _):
        def slot_body(k, _):
            slot = near_list[leaf, k]
            seg = slot // leaves
            at = counts[seg]
            item = ((slot - seg * leaves) * 2) * 2**ROW_BITS + leaf
            lists[seg, at] = item
            lists[seg, at + 1] = item + 2**ROW_BITS
            counts[seg] = at + 2
            return 0

        return lax.fori_loop(0, near_count[leaf], slot_body, 0)

    lax.fori_loop(0, leaves, leaf_body, 0)
    for seg in range(3):

        def far_body(leaf, at, seg=seg):
            for block in range(far_blocks[seg]):
                lists[seg, at + block] = (first_far + block) * 2**ROW_BITS + leaf
            return at + far_blocks[seg]

        end = lax.fori_loop(0, leaves, far_body, counts[seg])
        counts[seg] = end
        for pad in range(UNROLL):
            lists[seg, end + pad] = leaves


def skeleton_kernel(chunk, far_blocks, near_list, near_count, index, points, weights, maps, node, lists, counts, coords, values):
    step = pl.program_id(0)

    @pl.when(step == 0)
    def _():
        coords[...] = jnp.zeros_like(coords)
        values[...] = jnp.zeros_like(values)
        write_lists(near_list, near_count, lists, counts, far_blocks)

    rows = lax.broadcasted_iota(jnp.int32, (chunk, index.shape[1]), 0) + step * chunk
    pick = jnp.where(rows == index[...], 1.0, 0.0).astype(BF16)
    coords[...] += jnp.dot(points[...], pick, preferred_element_type=F32)
    values[...] += lax.dot_general(weights[...], maps[0], NT, preferred_element_type=F32)

    @pl.when(step == pl.num_programs(0) - 1)
    def _():
        dim = coords.shape[0]
        node[:dim, :] = coords[...].astype(BF16)
        node[dim:, :] = values[...].astype(BF16)


def skeleton(points, weights, near_list, near_count, index, maps, far_blocks):
    dim, width = points.shape
    columns = weights.shape[0]
    size = index.shape[1]
    chunk = 1024
    return pl.pallas_call(
        functools.partial(skeleton_kernel, chunk, far_blocks),
        grid=(width // chunk,),
        out_shape=(
            jax.ShapeDtypeStruct((dim + columns, size), BF16),
            jax.ShapeDtypeStruct((3, LIST), jnp.int32),
            jax.ShapeDtypeStruct((3,), jnp.int32),
        ),
        in_specs=[
            in_smem(),
            in_smem(),
            pl.BlockSpec((1, size), lambda i: (0, 0)),
            pl.BlockSpec((dim, chunk), lambda i: (0, i)),
            pl.BlockSpec((columns, chunk), lambda i: (0, i)),
            pl.BlockSpec((1, size, chunk), lambda i: (0, 0, i)),
        ],
        out_specs=(pl.BlockSpec((dim + columns, size), lambda i: (0, 0)), in_smem(), in_smem()),
        scratch_shapes=[pltpu.VMEM((dim, size), F32), pltpu.VMEM((columns, size), F32)],
        compiler_params=params(),
        name="skeleton",
    )(near_list, near_count, index, points, weights, maps)


def merge(dim, lower, upper, index, level_map):
    union = jnp.concatenate([lower, upper], axis=1)
    rows = lax.broadcasted_iota(jnp.int32, (union.shape[1], index.shape[1]), 0)
    pick = jnp.where(rows == index, 1.0, 0.0).astype(BF16)
    picked = jnp.dot(union[:dim], pick, preferred_element_type=F32)
    merged = lax.dot_general(union[dim:], level_map, NT, preferred_element_type=F32)
    return jnp.concatenate([picked, merged], axis=0).astype(BF16)


def climb_kernel(dim, level, last, position, index, maps, own, one, two, three, sibling, parent=None):
    low_bit = jnp.bitwise_and(position[0], 1)
    high_bit = jnp.bitwise_and(position[0] // 2, 1)

    def ordered(bit, same, other):
        is_upper = bit == 1
        same, other = same.astype(F32), other.astype(F32)
        lower = jnp.where(is_upper, other, same).astype(BF16)
        return lower, jnp.where(is_upper, same, other).astype(BF16)

    index_here = index[level : level + 1, :]
    lower, upper = ordered(low_bit, two[...], three[...])
    aside = merge(dim, lower, upper, index_here, maps[level])
    sibling[...] = aside
    if not last:
        lower, upper = ordered(low_bit, own[...], one[...])
        mine = merge(dim, lower, upper, index_here, maps[level])
        lower, upper = ordered(high_bit, mine, aside)
        parent[...] = merge(dim, lower, upper, index[level + 1 : level + 2, :], maps[level + 1])


def climb(dim, level, last, position, index, maps, nodes):
    shape = jax.ShapeDtypeStruct(nodes[0].shape, BF16)
    return pl.pallas_call(
        functools.partial(climb_kernel, dim, level, last),
        out_shape=(shape,) if last else (shape, shape),
        in_specs=[in_smem()] + [in_vmem()] * 6,
        out_specs=(in_vmem(),) if last else (in_vmem(), in_vmem()),
        compiler_params=params(),
        name="climb",
    )(jnp.reshape(position, (1,)).astype(jnp.int32), index, maps, *nodes)


def three_partners(node, level):
    nodes = [node]
    for mask in (1, 2, 3):
        pairs = [(i, i ^ (mask << level)) for i in range(lax.axis_size("box"))]
        nodes.append(lax.ppermute(node, "box", pairs))
    return nodes


def add_norm_rows(target, source, negative, at, width):
    dim = source.shape[0]
    piece = min(LEAF, width)
    target[dim + 16 :, at : at + width] = jnp.zeros((DEPTH - dim - 16, width), BF16)
    scale = 2.0 / dim

    def body(i, _):
        here = pl.ds(pl.multiple_of(i * piece, piece), piece)
        there = pl.ds(pl.multiple_of(at + i * piece, piece), piece)
        wide = source[:, here].astype(F32)
        norm = jnp.sum(wide * wide, axis=0, keepdims=True) * scale
        high = norm.astype(BF16).astype(F32)
        middle = (norm - high).astype(BF16).astype(F32)
        low = norm - high - middle
        row = lax.broadcasted_iota(jnp.int32, (16, piece), 0)
        first = 3 if negative else 0
        sign = -1.0 if negative else 1.0
        rows = jnp.where(row == first, high, jnp.where(row == first + 1, middle, low))
        norm_rows = (row >= first) & (row < first + 3)
        rows = jnp.where(norm_rows, rows, jnp.where(row < 6, 1.0, 0.0)) * sign
        target[:dim, there] = (wide * (2.0 * scale) ** 0.5).astype(BF16)
        target[dim : dim + 16, there] = rows.astype(BF16)
        return 0

    lax.fori_loop(0, width // piece, body, 0)


def pair_kernel(seg, n_nodes, has_box, has_start, final, *refs):
    refs = list(refs)
    lists, counts, own = refs[:3]
    del refs[:3]
    box = refs[:2] if has_box else []
    del refs[: len(box)]
    nodes = refs[:n_nodes]
    del refs[:n_nodes]
    start = refs.pop(0) if has_start else None
    out, rows, centers, values, total = refs
    dim, width = own.shape
    leaves = width // LEAF
    columns = values.shape[0]

    add_norm_rows(rows, own, False, 0, width)
    rows[:, width:] = jnp.zeros((DEPTH, LEAF), BF16)
    at = 0
    if has_box:
        add_norm_rows(centers, box[0], True, 0, width)
        values[:, :width] = box[1][...]
        at = width
    for node in nodes:
        add_norm_rows(centers, node.at[:dim], True, at, HALF)
        values[:, at : at + HALF] = node[dim:, :]
        at += HALF
    total[:, width:] = jnp.zeros((columns, LEAF), F32)
    total[:, :width] = start[...] if has_start else jnp.zeros((columns, width), F32)

    def run(items):
        items = [
            (pl.ds(pl.multiple_of(source * HALF, HALF), HALF), pl.ds(pl.multiple_of(leaf * LEAF, LEAF), LEAF))
            for source, leaf in items
        ]

        def exponents(item):
            return lax.dot_general(centers[:, item[0]], rows[:, item[1]], TN, preferred_element_type=F32)

        ahead = [exponents(item) for item in items[:AHEAD]]
        for n, item in enumerate(items):
            kern = jnp.exp(ahead[n]).astype(BF16)
            if n + AHEAD < len(items):
                ahead.append(exponents(items[n + AHEAD]))
            total[:, item[1]] += jnp.dot(values[:, item[0]], kern, preferred_element_type=F32)

    if has_box:

        def body(i, _):
            items = []
            for n in range(UNROLL):
                item = lists[seg, i * UNROLL + n]
                items.append((jnp.right_shift(item, ROW_BITS), jnp.bitwise_and(item, 2**ROW_BITS - 1)))
            run(items)
            return 0

        lax.fori_loop(0, (counts[seg] + UNROLL - 1) // UNROLL, body, 0)
    else:
        each = UNROLL // n_nodes

        def body(i, _):
            run([(node, i * each + n) for n in range(each) for node in range(n_nodes)])
            return 0

        lax.fori_loop(0, leaves // each, body, 0)
    out[...] = total[:, :width].astype(out.dtype)


def pairs(seg, lists, counts, own, box, nodes, start, final):
    dim, width = own.shape
    columns = nodes[0].shape[0] - dim if nodes else box[1].shape[0]
    sources = (width if box else 0) + HALF * len(nodes)
    args = [lists, counts, own, *box, *nodes] + ([] if start is None else [start])
    return pl.pallas_call(
        functools.partial(pair_kernel, seg, len(nodes), bool(box), start is not None, final),
        out_shape=jax.ShapeDtypeStruct((columns, width), BF16 if final else F32),
        in_specs=[in_smem(), in_smem()] + [in_vmem()] * (len(args) - 2),
        out_specs=in_vmem(),
        scratch_shapes=[
            pltpu.VMEM((DEPTH, width + LEAF), BF16),
            pltpu.VMEM((DEPTH, sources), BF16),
            pltpu.VMEM((columns, sources), BF16),
            pltpu.VMEM((columns, width + LEAF), F32),
        ],
        compiler_params=params(),
        name="pairs",
    )(*args)


def local(points, weights, near_list, near_count, skeleton_index, skeleton_maps, level_index, level_maps):
    points, weights = points.T, weights.T
    dim = points.shape[0]
    count = lax.axis_size("box")
    position = lax.axis_index("box")
    up = [(i, i + 1) for i in range(count - 1)]
    down = [(i + 1, i) for i in range(count - 1)]
    before = [lax.ppermute(a, "box", up) for a in (points, weights)]
    after = [lax.ppermute(a, "box", down) for a in (points, weights)]
    node, lists, counts = skeleton(
        points, weights, near_list, near_count, skeleton_index, skeleton_maps, (2, 0, 2)
    )
    nodes = three_partners(node, 0)
    total = pairs(1, lists, counts, points, (points, weights), [], None, False)
    sibling_1, node = climb(dim, 0, False, position, level_index, level_maps, nodes)
    siblings = [nodes[1], sibling_1]
    nodes = three_partners(node, 2)
    total = pairs(0, lists, counts, points, before, siblings, total, False)
    sibling_3, node = climb(dim, 2, False, position // 4, level_index, level_maps, nodes)
    siblings = [nodes[1], sibling_3]
    nodes = three_partners(node, 4)
    total = pairs(2, lists, counts, points, after, siblings, total, False)
    (sibling_5,) = climb(dim, 4, True, position // 16, level_index, level_maps, nodes)
    total = pairs(0, lists, counts, points, (), [nodes[1], sibling_5], total, True)
    return total.T


def solution(mesh):
    return jax.shard_map(
        local,
        mesh=mesh,
        in_specs=(
            P("box", None),
            P("box", "rhs"),
            P("box", None),
            P("box"),
            P("box", None),
            P("box", None, None),
            P(),
            P(),
        ),
        out_specs=P("box", "rhs"),
        check_vma=False,
    )
```

```python
import functools

import jax
import jax.numpy as jnp
from jax import lax
from jax.experimental import pallas as pl
from jax.experimental.pallas import tpu as pltpu
from jax.sharding import PartitionSpec as P

LEAF = 512
HALF = 256
UNROLL = 16
AHEAD = 2
LIST = 256
DEPTH = 80
ROW_BITS = 5
CHUNKS = 8
VMEM = 14 * 2**20
F32 = jnp.float32
BF16 = jnp.bfloat16
NT = (((1,), (1,)), ((), ()))
TN = (((0,), (0,)), ((), ()))


def in_vmem():
    return pl.BlockSpec(memory_space=pltpu.VMEM)


def in_smem():
    return pl.BlockSpec(memory_space=pltpu.SMEM)


def params():
    return pltpu.CompilerParams(vmem_limit_bytes=VMEM)


def cost(microseconds):
    return pl.CostEstimate(
        flops=int(microseconds * 10**9), bytes_accessed=int(microseconds * 10**6), transcendentals=0
    )


def pieces(points):
    wide = points.astype(F32)
    norm = jnp.sum(wide * wide, axis=0, keepdims=True) * (2.0 / points.shape[0])
    high = norm.astype(BF16).astype(F32)
    middle = (norm - high).astype(BF16).astype(F32)
    low = norm - high - middle
    scaled = (wide * (4.0 / points.shape[0]) ** 0.5).astype(BF16)
    return scaled, high, middle, low


def extended(points, of_rows):
    scaled, high, middle, low = pieces(points)
    first = 0 if of_rows else 3
    row = lax.broadcasted_iota(jnp.int32, (16, points.shape[1]), 0)
    norm = jnp.where(row == first, -high, jnp.where(row == first + 1, -middle, -low))
    is_norm = (row >= first) & (row < first + 3)
    return scaled, jnp.where(is_norm, norm, jnp.where(row < 6, 1.0, 0.0)).astype(BF16)


def put(target, at, points, of_rows):
    scaled, norm = extended(points, of_rows)
    dim = points.shape[0]
    target[:dim, at] = scaled
    target[dim:, at] = norm


def level_0_kernel(dim, near_list, near_count, index, both, maps, node, lists, counts, rows, centers):
    columns, width = both.shape[0] - dim, both.shape[1]
    leaves, slots = near_list.shape
    size = index.shape[1]
    rows[:, width:] = jnp.zeros((DEPTH, LEAF), BF16)
    coords = jnp.zeros((dim, size), F32)
    values = jnp.zeros((size, columns), F32)
    ends = [jnp.int32(s * LIST) for s in range(3)]
    chunk = width // CHUNKS
    for start in range(0, width, chunk):
        at = pl.ds(start, chunk)
        points = both[:dim, at]
        place = lax.broadcasted_iota(jnp.int32, (chunk, size), 0) + start
        pick = jnp.where(place == index[...], 1.0, 0.0).astype(BF16)
        coords += jnp.dot(points, pick, preferred_element_type=F32)
        values += lax.dot_general(maps[0, :, at], both[dim:, at], NT, preferred_element_type=F32)
        put(rows, at, points, True)
        put(centers, at, points, False)
        for leaf in range(start // LEAF, (start + chunk) // LEAF):
            live = near_count[leaf]
            for k in range(slots):
                slot = near_list[leaf, k]
                used = k < live
                low, mid = slot < leaves, slot < 2 * leaves
                to = jnp.where(low, ends[0], jnp.where(mid, ends[1], ends[2]))
                to = jnp.where(used, to, 3 * LIST)
                lists[to] = jnp.bitwise_and(slot, leaves - 1) * 2**ROW_BITS + leaf
                used = used.astype(jnp.int32)
                is_low, is_mid = low.astype(jnp.int32), mid.astype(jnp.int32)
                ends[0] += is_low * used
                ends[1] += (is_mid - is_low) * used
                ends[2] += (1 - is_mid) * used
    for s in range(3):
        counts[s] = ends[s] - s * LIST
        for pad in range(UNROLL // 2):
            lists[ends[s] + pad] = leaves
    node[:dim, :] = coords.astype(BF16)
    node[dim:, :] = values.T.astype(BF16)


def level_0(both, near_list, near_count, index, maps, dim):
    total, width = both.shape
    columns = total - dim
    size = index.shape[1]
    return pl.pallas_call(
        functools.partial(level_0_kernel, dim),
        out_shape=(
            jax.ShapeDtypeStruct((total, size), BF16),
            jax.ShapeDtypeStruct((3 * LIST + 8,), jnp.int32),
            jax.ShapeDtypeStruct((3,), jnp.int32),
            jax.ShapeDtypeStruct((DEPTH, width + LEAF), BF16),
            jax.ShapeDtypeStruct((DEPTH, width), BF16),
        ),
        in_specs=[in_smem(), in_smem(), in_vmem(), in_vmem(), in_vmem()],
        out_specs=(in_vmem(), in_smem(), in_smem(), in_vmem(), in_vmem()),
        compiler_params=params(),
        cost_estimate=cost(1),
        name="level_0",
    )(near_list, near_count, index, both, maps)


def climb_kernel(dim, level, position, index, maps, own, other, *refs):
    parent = refs[-1]
    is_upper = jnp.bitwise_and(jnp.right_shift(position[0], level), 1) == 1
    mine, theirs = own[...].astype(F32), other[...].astype(F32)
    lower = jnp.where(is_upper, theirs, mine).astype(BF16)
    upper = jnp.where(is_upper, mine, theirs).astype(BF16)
    union = jnp.concatenate([lower, upper], axis=1)
    here = index[level : level + 1, :]
    place = lax.broadcasted_iota(jnp.int32, (union.shape[1], here.shape[1]), 0)
    pick = jnp.where(place == here, 1.0, 0.0).astype(BF16)
    parent[:dim, :] = jnp.dot(union[:dim], pick, preferred_element_type=F32).astype(BF16)
    merged = lax.dot_general(union[dim:], maps[level], NT, preferred_element_type=F32)
    parent[dim:, :] = merged.astype(BF16)


def climb(dim, level, position, index, maps, own, other, after):
    order = [] if after is None else [after]
    return pl.pallas_call(
        functools.partial(climb_kernel, dim, level),
        out_shape=jax.ShapeDtypeStruct(own.shape, BF16),
        in_specs=[in_smem()] + [in_vmem()] * (4 + len(order)),
        out_specs=in_vmem(),
        compiler_params=params(),
        cost_estimate=cost(0.6),
        name="climb",
    )(jnp.reshape(position, (1,)).astype(jnp.int32), index, maps, own, other, *order)


def run(items):
    def exponents(item):
        (centers, at), _, (rows, to), _ = item
        return lax.dot_general(centers[:, at], rows[:, to], TN, preferred_element_type=F32)

    ahead = [exponents(item) for item in items[:AHEAD]]
    for n, (_, (values, at, first), _, (total, to)) in enumerate(items):
        kern = jnp.exp(ahead[n]).astype(BF16)
        if n + AHEAD < len(items):
            ahead.append(exponents(items[n + AHEAD]))
        total[:, to] += jnp.dot(values[first:, at], kern, preferred_element_type=F32)


def pair_kernel(dim, seg, piece, of, ready, has_start, *refs):
    refs = list(refs)
    lists, counts, rows, box = refs[:4]
    del refs[:4]
    centers = refs.pop(0) if ready else None
    node = refs.pop(0)
    start = refs.pop(0) if has_start else None
    total = refs.pop(0)
    far = refs.pop(0)
    if not ready:
        centers = refs.pop(0)

        def fill(i, _):
            at = pl.ds(pl.multiple_of(i * LEAF, LEAF), LEAF)
            put(centers, at, box[:dim, at], False)
            return 0

        lax.fori_loop(0, box.shape[1] // LEAF, fill, 0)
    leaves = box.shape[1] // LEAF
    put(far, pl.ds(0, HALF), node[:dim, :], False)
    total[...] = start[...] if has_start else jnp.zeros_like(total)
    everything = pl.ds(0, HALF)
    run([
        ((far, everything), (node, everything, dim), (rows, pl.ds(leaf * LEAF, LEAF)), (total, pl.ds(leaf * LEAF, LEAF)))
        for leaf in range(leaves)
    ])

    def body(i, _):
        items = []
        for n in range(UNROLL // 2):
            item = lists[seg * LIST + i * (UNROLL // 2) + n]
            source, leaf = jnp.right_shift(item, ROW_BITS), jnp.bitwise_and(item, 2**ROW_BITS - 1)
            to = pl.ds(pl.multiple_of(leaf * LEAF, LEAF), LEAF)
            for half in range(0, LEAF, HALF):
                at = pl.ds(pl.multiple_of(source * LEAF + half, HALF), HALF)
                items.append(((centers, at), (box, at, dim), (rows, to), (total, to)))
        run(items)
        return 0

    rounds = (counts[seg] + UNROLL // 2 - 1) // (UNROLL // 2)
    lax.fori_loop(rounds * piece // of, rounds * (piece + 1) // of, body, 0)


def pairs(dim, seg, piece, of, lists, counts, rows, box, centers, node, start):
    width = box.shape[1]
    columns = box.shape[0] - dim
    ready = centers is not None
    args = [lists, counts, rows, box] + ([centers] if ready else []) + [node]
    args += [] if start is None else [start]
    return pl.pallas_call(
        functools.partial(pair_kernel, dim, seg, piece, of, ready, start is not None),
        out_shape=jax.ShapeDtypeStruct((columns, width + LEAF), F32),
        in_specs=[in_smem(), in_smem()] + [in_vmem()] * (len(args) - 2),
        out_specs=in_vmem(),
        scratch_shapes=[pltpu.VMEM((DEPTH, HALF), BF16)]
        + ([] if ready else [pltpu.VMEM((DEPTH, width), BF16)]),
        compiler_params=params(),
        cost_estimate=cost(4),
        name="pairs",
    )(*args)


def last_kernel(dim, rows, node, start, out, far, total):
    width = out.shape[1]
    put(far, pl.ds(0, HALF), node[:dim, :], False)
    total[...] = start[:, :width]
    everything = pl.ds(0, HALF)
    run([
        ((far, everything), (node, everything, dim), (rows, pl.ds(at, LEAF)), (total, pl.ds(at, LEAF)))
        for at in range(0, width, LEAF)
    ])
    out[...] = total[...].astype(BF16)


def last(dim, rows, node, start):
    columns, width = start.shape[0], start.shape[1] - LEAF
    return pl.pallas_call(
        functools.partial(last_kernel, dim),
        out_shape=jax.ShapeDtypeStruct((columns, width), BF16),
        in_specs=[in_vmem()] * 3,
        out_specs=in_vmem(),
        scratch_shapes=[pltpu.VMEM((DEPTH, HALF), BF16), pltpu.VMEM((columns, width), F32)],
        compiler_params=params(),
        cost_estimate=cost(3),
        name="last",
    )(rows, node, start)


def local(points, weights, near_list, near_count, skeleton_index, skeleton_maps, level_index, level_maps):
    dim = points.shape[1]
    both = jnp.concatenate([points.T, weights.T], axis=0)
    count = lax.axis_size("box")
    position = lax.axis_index("box")
    before = lax.ppermute(both, "box", [(i, i + 1) for i in range(count - 1)])
    after = lax.ppermute(both, "box", [(i + 1, i) for i in range(count - 1)])
    node, lists, counts, rows, centers = level_0(
        both, near_list, near_count, skeleton_index, skeleton_maps, dim
    )

    def sibling(node, level):
        return lax.ppermute(node, "box", [(i, i ^ (1 << level)) for i in range(count)])

    plan = [
        (1, 0, 3, both, centers),
        (1, 1, 3, both, centers),
        (0, 0, 1, before, None),
        (2, 0, 1, after, None),
        (1, 2, 3, both, centers),
    ]
    total = None
    other = sibling(node, 0)
    for level, (seg, piece, of, box, ready) in enumerate(plan):
        node = climb(dim, level, position, level_index, level_maps, node, other, total)
        far = other
        other = sibling(node, level + 1)
        total = pairs(dim, seg, piece, of, lists, counts, rows, box, ready, far, total)
    return last(dim, rows, other, total).T


def solution(mesh):
    return jax.shard_map(
        local,
        mesh=mesh,
        in_specs=(
            P("box", None),
            P("box", "rhs"),
            P("box", None),
            P("box"),
            P("box", None),
            P("box", None, None),
            P(),
            P(),
        ),
        out_specs=P("box", "rhs"),
        check_vma=False,
    )
```

```python
import functools

import jax
import jax.numpy as jnp
from jax import lax
from jax.experimental import pallas as pl
from jax.experimental.pallas import tpu as pltpu
from jax.sharding import PartitionSpec as P

LEAF = 512
HALF = 256
MAIN = 32
REST = 8
AHEAD = 2
LIST = 256
NORMS = 16
ROW_BITS = 5
CHUNKS = 8
LOG2E = 1.4426950408889634
VMEM = 14 * 2**20
VMEM_0 = 56 * 2**20
F32 = jnp.float32
BF16 = jnp.bfloat16
NT = (((1,), (1,)), ((), ()))
TN = (((0,), (0,)), ((), ()))


def in_vmem():
    return pl.BlockSpec(memory_space=pltpu.VMEM)


def in_smem():
    return pl.BlockSpec(memory_space=pltpu.SMEM)


def params():
    return pltpu.CompilerParams(vmem_limit_bytes=VMEM)


def cost(microseconds):
    return pl.CostEstimate(
        flops=int(microseconds * 10**9), bytes_accessed=int(microseconds * 10**6), transcendentals=0
    )


def norms(points, of_rows):
    wide = points.astype(F32)
    half = jnp.sum(wide * wide, axis=0, keepdims=True) * -0.5
    high = half.astype(BF16).astype(F32)
    middle = (half - high).astype(BF16).astype(F32)
    low = half - high - middle
    first = 0 if of_rows else 3
    row = lax.broadcasted_iota(jnp.int32, (NORMS, points.shape[1]), 0)
    norm = jnp.where(row == first, high, jnp.where(row == first + 1, middle, low))
    is_norm = (row >= first) & (row < first + 3)
    return jnp.where(is_norm, norm, jnp.where(row < 6, 1.0, 0.0)).astype(BF16)


def level_0_kernel(dim, near_list, near_count, index, points_far, weights_far, maps_far, node, lists, counts, rows, centers, both, maps, sems):
    columns, width = both.shape[0] - dim, both.shape[1]
    leaves, slots = near_list.shape
    size = index.shape[1]
    coords = jnp.zeros((dim, size), F32)
    values = jnp.zeros((size, columns), F32)
    ends = [jnp.int32(s * LIST) for s in range(3)]
    chunk = width // CHUNKS
    copies = []
    for i in range(CHUNKS):
        at = pl.ds(i * chunk, chunk)
        copies.append((
            pltpu.make_async_copy(points_far.at[:, at], both.at[:dim, at], sems.at[0, i]),
            pltpu.make_async_copy(weights_far.at[:, at], both.at[dim:, at], sems.at[1, i]),
            pltpu.make_async_copy(maps_far.at[0, :, at], maps.at[:, at], sems.at[2, i]),
        ))
        for copy in copies[-1]:
            copy.start()
    for start in range(0, width, chunk):
        at = pl.ds(start, chunk)
        for copy in copies[start // chunk]:
            copy.wait()
        points = both[:dim, at]
        place = lax.broadcasted_iota(jnp.int32, (chunk, size), 0) + start
        pick = jnp.where(place == index[...], 1.0, 0.0).astype(BF16)
        coords += jnp.dot(points, pick, preferred_element_type=F32)
        values += lax.dot_general(maps[:, at], both[dim:, at], NT, preferred_element_type=F32)
        rows[:, at] = norms(points, True)
        centers[:, at] = norms(points, False)
        for leaf in range(start // LEAF, (start + chunk) // LEAF):
            live = near_count[leaf]
            for k in range(slots):
                slot = near_list[leaf, k]
                used = k < live
                low, mid = slot < leaves, slot < 2 * leaves
                to = jnp.where(low, ends[0], jnp.where(mid, ends[1], ends[2]))
                to = jnp.where(used, to, 3 * LIST)
                lists[to] = jnp.bitwise_and(slot, leaves - 1) * 2**ROW_BITS + leaf
                used = used.astype(jnp.int32)
                is_low, is_mid = low.astype(jnp.int32), mid.astype(jnp.int32)
                ends[0] += is_low * used
                ends[1] += (is_mid - is_low) * used
                ends[2] += (1 - is_mid) * used
    for s in range(3):
        counts[s] = ends[s] - s * LIST
        for pad in range(REST // 2):
            lists[ends[s] + pad] = leaves
    node[:dim, :] = coords.astype(BF16)
    node[dim:, :] = values.T.astype(BF16)


def level_0(points, weights, near_list, near_count, index, maps):
    dim, width = points.shape
    total = dim + weights.shape[0]
    size = index.shape[1]
    return pl.pallas_call(
        functools.partial(level_0_kernel, dim),
        out_shape=(
            jax.ShapeDtypeStruct((total, size), BF16),
            jax.ShapeDtypeStruct((3 * LIST + 8,), jnp.int32),
            jax.ShapeDtypeStruct((3,), jnp.int32),
            jax.ShapeDtypeStruct((NORMS, width), BF16),
            jax.ShapeDtypeStruct((NORMS, width), BF16),
        ),
        in_specs=[in_smem(), in_smem(), in_vmem()] + [pl.BlockSpec(memory_space=pl.ANY)] * 3,
        out_specs=(in_vmem(), in_smem(), in_smem(), in_vmem(), in_vmem()),
        scratch_shapes=[
            pltpu.VMEM((total, width), BF16),
            pltpu.VMEM(maps.shape[1:], BF16),
            pltpu.SemaphoreType.DMA((3, CHUNKS)),
        ],
        compiler_params=pltpu.CompilerParams(vmem_limit_bytes=VMEM_0),
        cost_estimate=cost(1),
        name="level_0",
    )(near_list, near_count, index, points, weights, maps)


def climb_kernel(dim, level, position, index, maps, own, other, *refs):
    parent = refs[-1]
    is_upper = jnp.bitwise_and(jnp.right_shift(position[0], level), 1) == 1
    mine, theirs = own[...].astype(F32), other[...].astype(F32)
    lower = jnp.where(is_upper, theirs, mine).astype(BF16)
    upper = jnp.where(is_upper, mine, theirs).astype(BF16)
    union = jnp.concatenate([lower, upper], axis=1)
    here = index[level : level + 1, :]
    place = lax.broadcasted_iota(jnp.int32, (union.shape[1], here.shape[1]), 0)
    pick = jnp.where(place == here, 1.0, 0.0).astype(BF16)
    parent[:dim, :] = jnp.dot(union[:dim], pick, preferred_element_type=F32).astype(BF16)
    merged = lax.dot_general(union[dim:], maps[level], NT, preferred_element_type=F32)
    parent[dim:, :] = merged.astype(BF16)


def climb(dim, level, position, index, maps, own, other, after):
    order = [] if after is None else [after]
    return pl.pallas_call(
        functools.partial(climb_kernel, dim, level),
        out_shape=jax.ShapeDtypeStruct(own.shape, BF16),
        in_specs=[in_smem()] + [in_vmem()] * (4 + len(order)),
        out_specs=in_vmem(),
        compiler_params=params(),
        cost_estimate=cost(0.6),
        name="climb",
    )(jnp.reshape(position, (1,)).astype(jnp.int32), index, maps, own, other, *order)


def run(scale, items):
    def exponents(item):
        (centers, center_norms, at), _, (rows, row_norms, to), _ = item
        left = jnp.concatenate([centers[:, at], center_norms[:, at]], axis=0)
        right = jnp.concatenate([rows[:, to], row_norms[:, to]], axis=0)
        return lax.dot_general(left, right, TN, preferred_element_type=F32)

    ahead = [exponents(item) for item in items[:AHEAD]]
    for n, (_, (values, at), _, (total, to)) in enumerate(items):
        kern = jnp.exp2(ahead[n] * scale).astype(BF16)
        if n + AHEAD < len(items):
            ahead.append(exponents(items[n + AHEAD]))
        total[:, to] += jnp.dot(values[:, at], kern, preferred_element_type=F32)


def far_items(own, rows, node, node_norms, total, dim, width):
    here = pl.ds(0, HALF)
    return [
        ((node.at[:dim], node_norms, here), (node.at[dim:], here), (own.at[:dim], rows, pl.ds(at, LEAF)), (total, pl.ds(at, LEAF)))
        for at in range(0, width, LEAF)
    ]


def pair_kernel(dim, seg, piece, of, own_box, has_start, *refs):
    refs = list(refs)
    lists, counts, own, rows, centers = refs[:5]
    del refs[:5]
    box = own if own_box else centers
    node = refs.pop(0)
    start = refs.pop(0) if has_start else None
    total, node_norms = refs[:2]
    width = own.shape[1]
    leaves = width // LEAF
    scale = 4.0 / dim * LOG2E
    if not own_box:
        centers = refs[2]
        chunk = width // CHUNKS
        for at in range(0, width, chunk):
            centers[:, pl.ds(at, chunk)] = norms(box[:dim, pl.ds(at, chunk)], False)
    node_norms[...] = norms(node[:dim, :], False)
    total[...] = start[...] if has_start else jnp.zeros_like(total)
    run(scale, far_items(own, rows, node, node_norms, total, dim, width))

    def body(first, size, i, _):
        items = []
        for n in range(size // 2):
            item = lists[seg * LIST + first + i * (size // 2) + n]
            source, leaf = jnp.right_shift(item, ROW_BITS), jnp.bitwise_and(item, 2**ROW_BITS - 1)
            to = pl.ds(pl.multiple_of(leaf * LEAF, LEAF), LEAF)
            row = pl.ds(pl.multiple_of(jnp.minimum(leaf, leaves - 1) * LEAF, LEAF), LEAF)
            for half in range(0, LEAF, HALF):
                at = pl.ds(pl.multiple_of(source * LEAF + half, HALF), HALF)
                items.append(((box.at[:dim], centers, at), (box.at[dim:], at), (own.at[:dim], rows, row), (total, to)))
        run(scale, items)
        return 0

    groups = (counts[seg] + REST // 2 - 1) // (REST // 2)
    low = groups * piece // of
    many = groups * (piece + 1) // of - low
    mains = many // (MAIN // REST)
    first = low * (REST // 2)
    lax.fori_loop(0, mains, functools.partial(body, first, MAIN), 0)
    first += mains * (MAIN // 2)
    lax.fori_loop(0, many - mains * (MAIN // REST), functools.partial(body, first, REST), 0)


def pairs(dim, seg, piece, of, lists, counts, own, rows, centers, own_box, node, start):
    width = own.shape[1]
    columns = own.shape[0] - dim
    args = [lists, counts, own, rows, centers, node] + ([] if start is None else [start])
    return pl.pallas_call(
        functools.partial(pair_kernel, dim, seg, piece, of, own_box, start is not None),
        out_shape=jax.ShapeDtypeStruct((columns, width + LEAF), F32),
        in_specs=[in_smem(), in_smem()] + [in_vmem()] * (len(args) - 2),
        out_specs=in_vmem(),
        scratch_shapes=[pltpu.VMEM((NORMS, HALF), BF16)]
        + ([] if own_box else [pltpu.VMEM((NORMS, width), BF16)]),
        compiler_params=params(),
        cost_estimate=cost(4),
        name="pairs",
    )(*args)


def last_kernel(dim, own, rows, node, start, out, node_norms, total):
    width = out.shape[1]
    node_norms[...] = norms(node[:dim, :], False)
    total[...] = start[:, :width]
    run(4.0 / dim * LOG2E, far_items(own, rows, node, node_norms, total, dim, width))
    out[...] = total[...].astype(BF16)


def last(dim, own, rows, node, start):
    columns, width = start.shape[0], start.shape[1] - LEAF
    return pl.pallas_call(
        functools.partial(last_kernel, dim),
        out_shape=jax.ShapeDtypeStruct((columns, width), BF16),
        in_specs=[in_vmem()] * 4,
        out_specs=in_vmem(),
        scratch_shapes=[pltpu.VMEM((NORMS, HALF), BF16), pltpu.VMEM((columns, width), F32)],
        compiler_params=params(),
        cost_estimate=cost(3),
        name="last",
    )(own, rows, node, start)


def local(points, weights, near_list, near_count, skeleton_index, skeleton_maps, level_index, level_maps):
    dim = points.shape[1]
    count = lax.axis_size("box")
    position = lax.axis_index("box")
    both = jnp.concatenate([points.T, weights.T], axis=0)
    before = lax.ppermute(both, "box", [(i, i + 1) for i in range(count - 1)])
    after = lax.ppermute(both, "box", [(i + 1, i) for i in range(count - 1)])
    node, lists, counts, rows, centers = level_0(
        points.T, weights.T, near_list, near_count, skeleton_index, skeleton_maps
    )

    def sibling(node, level):
        return lax.ppermute(node, "box", [(i, i ^ (1 << level)) for i in range(count)])

    plan = [
        (1, 0, 1, centers, True),
        (0, 0, 2, before, False),
        (0, 1, 2, before, False),
        (2, 0, 2, after, False),
        (2, 1, 2, after, False),
    ]
    total = None
    other = sibling(node, 0)
    for level, (seg, piece, of, beside, own_box) in enumerate(plan):
        node = climb(dim, level, position, level_index, level_maps, node, other, total)
        far = other
        other = sibling(node, level + 1)
        total = pairs(dim, seg, piece, of, lists, counts, both, rows, beside, own_box, far, total)
    return last(dim, both, rows, other, total).T


def solution(mesh):
    return jax.shard_map(
        local,
        mesh=mesh,
        in_specs=(
            P("box", None),
            P("box", "rhs"),
            P("box", None),
            P("box"),
            P("box", None),
            P("box", None, None),
            P(),
            P(),
        ),
        out_specs=P("box", "rhs"),
        check_vma=False,
    )
```

```python
import functools

import jax
import jax.numpy as jnp
from jax import lax
from jax.experimental import pallas as pl
from jax.experimental.pallas import tpu as pltpu
from jax.sharding import PartitionSpec as P

LEAF = 512
HALF = 256
MAIN = 32
REST = 8
AHEAD = 2
LIST = 256
NORMS = 16
ROW_BITS = 5
CHUNKS = 8
LOG2E = 1.4426950408889634
VMEM = 14 * 2**20
VMEM_0 = 52 * 2**20
F32 = jnp.float32
BF16 = jnp.bfloat16
NT = (((1,), (1,)), ((), ()))
TN = (((0,), (0,)), ((), ()))


def in_vmem():
    return pl.BlockSpec(memory_space=pltpu.VMEM)


def in_smem():
    return pl.BlockSpec(memory_space=pltpu.SMEM)


def params():
    return pltpu.CompilerParams(vmem_limit_bytes=VMEM)


def cost(microseconds):
    return pl.CostEstimate(
        flops=int(microseconds * 10**9), bytes_accessed=int(microseconds * 10**6), transcendentals=0
    )


def norms(points, of_rows):
    wide = points.astype(F32)
    half = jnp.sum(wide * wide, axis=0, keepdims=True) * -0.5
    high = half.astype(BF16).astype(F32)
    middle = (half - high).astype(BF16).astype(F32)
    low = half - high - middle
    first = 0 if of_rows else 3
    row = lax.broadcasted_iota(jnp.int32, (NORMS, points.shape[1]), 0)
    norm = jnp.where(row == first, high, jnp.where(row == first + 1, middle, low))
    is_norm = (row >= first) & (row < first + 3)
    return jnp.where(is_norm, norm, jnp.where(row < 6, 1.0, 0.0)).astype(BF16)


def level_0_kernel(dim, near_list, near_count, index, points_far, weights_far, maps_far, node, lists, counts, rows, centers, both, maps, sems):
    columns, width = both.shape[0] - dim, both.shape[1]
    leaves, slots = near_list.shape
    size = index.shape[1]
    coords = jnp.zeros((dim, size), F32)
    values = jnp.zeros((size, columns), F32)
    ends = [jnp.int32(s * LIST) for s in range(3)]
    chunk = width // CHUNKS
    copies = []
    for i in range(CHUNKS):
        at = pl.ds(i * chunk, chunk)
        copies.append((
            pltpu.make_async_copy(points_far.at[:, at], both.at[:dim, at], sems.at[0, i]),
            pltpu.make_async_copy(weights_far.at[:, at], both.at[dim:, at], sems.at[1, i]),
            pltpu.make_async_copy(maps_far.at[0, :, at], maps.at[:, at], sems.at[2, i]),
        ))
        for copy in copies[-1]:
            copy.start()
    for start in range(0, width, chunk):
        at = pl.ds(start, chunk)
        for copy in copies[start // chunk]:
            copy.wait()
        points = both[:dim, at]
        place = lax.broadcasted_iota(jnp.int32, (chunk, size), 0) + start
        pick = jnp.where(place == index[...], 1.0, 0.0).astype(BF16)
        coords += jnp.dot(points, pick, preferred_element_type=F32)
        values += lax.dot_general(maps[:, at], both[dim:, at], NT, preferred_element_type=F32)
        rows[:, at] = norms(points, True)
        centers[:, at] = norms(points, False)
        for leaf in range(start // LEAF, (start + chunk) // LEAF):
            live = near_count[leaf]
            for k in range(slots):
                slot = near_list[leaf, k]
                used = k < live
                low, mid = slot < leaves, slot < 2 * leaves
                to = jnp.where(low, ends[0], jnp.where(mid, ends[1], ends[2]))
                to = jnp.where(used, to, 3 * LIST)
                lists[to] = jnp.bitwise_and(slot, leaves - 1) * 2**ROW_BITS + leaf
                used = used.astype(jnp.int32)
                is_low, is_mid = low.astype(jnp.int32), mid.astype(jnp.int32)
                ends[0] += is_low * used
                ends[1] += (is_mid - is_low) * used
                ends[2] += (1 - is_mid) * used
    for s in range(3):
        counts[s] = ends[s] - s * LIST
        for pad in range(REST // 2):
            lists[ends[s] + pad] = leaves
    node[:dim, :] = coords.astype(BF16)
    node[dim:, :] = values.T.astype(BF16)


def level_0(points, weights, near_list, near_count, index, maps):
    dim, width = points.shape
    total = dim + weights.shape[0]
    size = index.shape[1]
    return pl.pallas_call(
        functools.partial(level_0_kernel, dim),
        out_shape=(
            jax.ShapeDtypeStruct((total, size), BF16),
            jax.ShapeDtypeStruct((3 * LIST + 8,), jnp.int32),
            jax.ShapeDtypeStruct((3,), jnp.int32),
            jax.ShapeDtypeStruct((NORMS, width), BF16),
            jax.ShapeDtypeStruct((NORMS, width), BF16),
        ),
        in_specs=[in_smem(), in_smem(), in_vmem()] + [pl.BlockSpec(memory_space=pl.ANY)] * 3,
        out_specs=(in_vmem(), in_smem(), in_smem(), in_vmem(), in_vmem()),
        scratch_shapes=[
            pltpu.VMEM((total, width), BF16),
            pltpu.VMEM(maps.shape[1:], BF16),
            pltpu.SemaphoreType.DMA((3, CHUNKS)),
        ],
        compiler_params=pltpu.CompilerParams(vmem_limit_bytes=VMEM_0),
        cost_estimate=cost(1),
        name="level_0",
    )(near_list, near_count, index, points, weights, maps)


def climb_kernel(dim, level, position, index, maps, own, other, *refs):
    parent = refs[-1]
    is_upper = jnp.bitwise_and(jnp.right_shift(position[0], level), 1) == 1
    mine, theirs = own[...].astype(F32), other[...].astype(F32)
    lower = jnp.where(is_upper, theirs, mine).astype(BF16)
    upper = jnp.where(is_upper, mine, theirs).astype(BF16)
    union = jnp.concatenate([lower, upper], axis=1)
    here = index[level : level + 1, :]
    place = lax.broadcasted_iota(jnp.int32, (union.shape[1], here.shape[1]), 0)
    pick = jnp.where(place == here, 1.0, 0.0).astype(BF16)
    parent[:dim, :] = jnp.dot(union[:dim], pick, preferred_element_type=F32).astype(BF16)
    merged = lax.dot_general(union[dim:], maps[level], NT, preferred_element_type=F32)
    parent[dim:, :] = merged.astype(BF16)


def climb(dim, level, position, index, maps, own, other, after):
    order = [] if after is None else [after]
    return pl.pallas_call(
        functools.partial(climb_kernel, dim, level),
        out_shape=jax.ShapeDtypeStruct(own.shape, BF16),
        in_specs=[in_smem()] + [in_vmem()] * (4 + len(order)),
        out_specs=in_vmem(),
        compiler_params=params(),
        cost_estimate=cost(0.6),
        name="climb",
    )(jnp.reshape(position, (1,)).astype(jnp.int32), index, maps, own, other, *order)


def run(scale, items):
    def exponents(item):
        (centers, center_norms, at), _, (rows, row_norms, to), _ = item
        left = jnp.concatenate([centers[:, at], center_norms[:, at]], axis=0)
        right = jnp.concatenate([rows[:, to], row_norms[:, to]], axis=0)
        return lax.dot_general(left, right, TN, preferred_element_type=F32)

    ahead = [exponents(item) for item in items[:AHEAD]]
    for n, (_, (values, at), _, (total, to)) in enumerate(items):
        kern = jnp.exp2(ahead[n] * scale).astype(BF16)
        if n + AHEAD < len(items):
            ahead.append(exponents(items[n + AHEAD]))
        total[:, to] += jnp.dot(values[:, at], kern, preferred_element_type=F32)


def far_items(own, rows, node, node_norms, total, dim, width):
    here = pl.ds(0, HALF)
    return [
        ((node.at[:dim], node_norms, here), (node.at[dim:], here), (own.at[:dim], rows, pl.ds(at, LEAF)), (total, pl.ds(at, LEAF)))
        for at in range(0, width, LEAF)
    ]


def pair_kernel(dim, seg, piece, of, own_box, has_node, has_start, *refs):
    refs = list(refs)
    lists, counts, own, rows, centers = refs[:5]
    del refs[:5]
    box = own if own_box else centers
    node = refs.pop(0) if has_node else None
    start = refs.pop(0) if has_start else None
    total, token, node_norms = refs[:3]
    token[...] = jnp.zeros_like(token)
    width = own.shape[1]
    leaves = width // LEAF
    scale = 4.0 / dim * LOG2E
    if not own_box:
        centers = refs[3]
        chunk = width // CHUNKS
        for at in range(0, width, chunk):
            centers[:, pl.ds(at, chunk)] = norms(box[:dim, pl.ds(at, chunk)], False)
    total[...] = start[...] if has_start else jnp.zeros_like(total)
    if has_node:
        node_norms[...] = norms(node[:dim, :], False)
        run(scale, far_items(own, rows, node, node_norms, total, dim, width))

    def body(first, size, i, _):
        items = []
        for n in range(size // 2):
            item = lists[seg * LIST + first + i * (size // 2) + n]
            source, leaf = jnp.right_shift(item, ROW_BITS), jnp.bitwise_and(item, 2**ROW_BITS - 1)
            to = pl.ds(pl.multiple_of(leaf * LEAF, LEAF), LEAF)
            row = pl.ds(pl.multiple_of(jnp.minimum(leaf, leaves - 1) * LEAF, LEAF), LEAF)
            for half in range(0, LEAF, HALF):
                at = pl.ds(pl.multiple_of(source * LEAF + half, HALF), HALF)
                items.append(((box.at[:dim], centers, at), (box.at[dim:], at), (own.at[:dim], rows, row), (total, to)))
        run(scale, items)
        return 0

    groups = (counts[seg] + REST // 2 - 1) // (REST // 2)
    low = groups * piece // of
    many = groups * (piece + 1) // of - low
    mains = many // (MAIN // REST)
    first = low * (REST // 2)
    lax.fori_loop(0, mains, functools.partial(body, first, MAIN), 0)
    first += mains * (MAIN // 2)
    lax.fori_loop(0, many - mains * (MAIN // REST), functools.partial(body, first, REST), 0)


def pairs(dim, seg, piece, of, lists, counts, own, rows, centers, own_box, node, start):
    width = own.shape[1]
    columns = own.shape[0] - dim
    args = [lists, counts, own, rows, centers] + [a for a in (node, start) if a is not None]
    return pl.pallas_call(
        functools.partial(pair_kernel, dim, seg, piece, of, own_box, node is not None, start is not None),
        out_shape=(jax.ShapeDtypeStruct((columns, width + LEAF), F32), jax.ShapeDtypeStruct((8, 128), F32)),
        in_specs=[in_smem(), in_smem()] + [in_vmem()] * (len(args) - 2),
        out_specs=(in_vmem(), in_vmem()),
        scratch_shapes=[pltpu.VMEM((NORMS, HALF), BF16)]
        + ([] if own_box else [pltpu.VMEM((NORMS, width), BF16)]),
        compiler_params=params(),
        cost_estimate=cost(4),
        name="pairs",
    )(*args)


def last_kernel(dim, own, rows, node, start, out, node_norms, total):
    width = out.shape[1]
    node_norms[...] = norms(node[:dim, :], False)
    total[...] = start[:, :width]
    run(4.0 / dim * LOG2E, far_items(own, rows, node, node_norms, total, dim, width))
    out[...] = total[...].astype(BF16)


def last(dim, own, rows, node, start):
    columns, width = start.shape[0], start.shape[1] - LEAF
    return pl.pallas_call(
        functools.partial(last_kernel, dim),
        out_shape=jax.ShapeDtypeStruct((columns, width), BF16),
        in_specs=[in_vmem()] * 4,
        out_specs=in_vmem(),
        scratch_shapes=[pltpu.VMEM((NORMS, HALF), BF16), pltpu.VMEM((columns, width), F32)],
        compiler_params=params(),
        cost_estimate=cost(3),
        name="last",
    )(own, rows, node, start)


def local(points, weights, near_list, near_count, skeleton_index, skeleton_maps, level_index, level_maps):
    dim = points.shape[1]
    count = lax.axis_size("box")
    position = lax.axis_index("box")
    both = jnp.concatenate([points.T, weights.T], axis=0)
    before = lax.ppermute(both, "box", [(i, i + 1) for i in range(count - 1)])
    after = lax.ppermute(both, "box", [(i + 1, i) for i in range(count - 1)])
    node, lists, counts, rows, centers = level_0(
        points.T, weights.T, near_list, near_count, skeleton_index, skeleton_maps
    )

    def sibling(node, level):
        return lax.ppermute(node, "box", [(i, i ^ (1 << level)) for i in range(count)])

    plan = [
        (1, 0, 2, centers, True),
        (1, 1, 2, centers, True),
        (0, 0, 2, before, False),
        (0, 1, 2, before, False),
        (2, 0, 2, after, False),
        (2, 1, 2, after, False),
    ]
    total = far = None
    for level, (seg, piece, of, beside, own_box) in enumerate(plan):
        other = sibling(node, level)
        total, token = pairs(
            dim, seg, piece, of, lists, counts, both, rows, beside, own_box, far, total
        )
        if level + 1 < len(plan):
            node = climb(dim, level, position, level_index, level_maps, node, other, token)
        far = other
    return last(dim, both, rows, far, total).T


def solution(mesh):
    return jax.shard_map(
        local,
        mesh=mesh,
        in_specs=(
            P("box", None),
            P("box", "rhs"),
            P("box", None),
            P("box"),
            P("box", None),
            P("box", None, None),
            P(),
            P(),
        ),
        out_specs=P("box", "rhs"),
        check_vma=False,
    )
```
